128 devices in a mesh: row: 8 (over y, z_lo), col: 16 (over x, z_hi, core).
Axes of the slice: x: 4, y: 4, z: 4 (z_hi: 2, z_lo: 2; z = z_hi * 2 + z_lo), core: 2. Of those that a mesh axis runs over, the one named last changes fastest.
Arguments:
- tokens: bfloat16 [1024, 12288], P('col', 'row'), may hold values from -1.5 to 1.5
- weight: bfloat16 [12288, 49152], P('row', 'col'), may hold values from -0.0546875 to 0.0546875
- pre_act: bfloat16 [1024, 49152], P('row', 'col'), may hold values from -6 to 6
- upstream: bfloat16 [1024, 49152], P('row', 'col'), may hold values from -6 to 6
Outputs:
- input_grad: bfloat16 [1024, 12288], P('col', 'row')
- weight_grad: bfloat16 [12288, 49152], P('row', 'col')
The draws below stay inside these ranges and needn't reach their ends.
All inputs are finite; a program needn't handle non-finite values.
Results may differ from the reference program's by a relative error of at most 0.0049.
Values may be sent and summed in bfloat16 or wider, within the bound.
No kernel may reach another device: no remote copies, remote signals or barrier semaphores. Data moves between devices by JAX's collectives and lax.ppermute only.
A program may use at most 128 MiB of HBM per device.

```python
import math
import jax
import jax.numpy as jnp

D = 12288
FF = 49152
TOKENS = 1024


def strengthened(values, rng, source, target, parts, factor):
    owner, partner = [(jnp.arange(values.shape[axis_at]) // (values.shape[axis_at] // parts)).reshape([-1 if axis == axis_at else 1 for axis in range(values.ndim)]) for axis_at in (source, target)]
    chosen = jax.random.permutation(rng, parts)[partner]
    strong = (owner == chosen) | (owner == (partner + parts // 2) % parts)
    return jnp.where(strong, factor * values, values)


def block_levels(own_key, extent, shards, smallest, high):
    loudness, own = 1.0, jax.random.fold_in(own_key, 6)
    for position, parts in shards:
        steps = jnp.exp(jax.random.uniform(jax.random.fold_in(own, position), (parts,), jnp.float32, smallest / len(shards), high / len(shards)))
        loudness = loudness * jnp.repeat(steps, extent[position] // parts).reshape([-1 if axis == position else 1 for axis in range(len(extent))])
    return loudness


def bell_draw(rng, shape, width, bound, shards=(), kind=jnp.bfloat16):
    array = width * jax.random.normal(rng, shape, jnp.float32)
    if shards:
        array = array * block_levels(rng, shape, shards, -0.22, 0.18)
    return jnp.clip(array, -bound, bound).astype(kind)


def heavy_noise(stream_key, dims, width, reach, split, heavy, kind=jnp.bfloat16):
    array = width * jax.random.normal(stream_key, dims, jnp.float32)
    if split:
        array = array * block_levels(stream_key, dims, split, -0.22, 0.18)
    return jnp.clip(strengthened(array, jax.random.fold_in(stream_key, 3), *heavy), -reach, reach).astype(kind)


def setup_inputs(seed: int = 0) -> dict:
    splits = jax.random.split(jax.random.key(seed), 5)
    tokens = bell_draw(splits[0], (TOKENS, D), 0.25, 1.5, ((0, 16), (1, 8)))
    weight = bell_draw(splits[1], (D, FF), D ** -0.5, 0.0546875, ((0, 8), (1, 16)))
    pre_act = bell_draw(splits[2], (TOKENS, FF), 1.0, 6.0, ((0, 8), (1, 16)))
    upstream = heavy_noise(splits[3], (TOKENS, FF), 1.0, 6.0, ((0, 8), (1, 16)), (1, 0, 16, 2.0))
    return {"tokens": tokens, "weight": weight, "pre_act": pre_act, "upstream": upstream}


def gelu_slope(value):
    scale = math.sqrt(2.0 / math.pi)
    inner = scale * (value + 0.044715 * value * value * value)
    tangent = jnp.tanh(inner)
    return 0.5 * (1.0 + tangent) + 0.5 * value * (1.0 - tangent * tangent) * scale * (1.0 + 3.0 * 0.044715 * value * value)

def reference(tokens, weight, pre_act, upstream):
    grad_hidden = (upstream.astype(jnp.float32) * gelu_slope(pre_act.astype(jnp.float32))).astype(jnp.bfloat16)
    input_grad = jnp.dot(grad_hidden, weight.T, preferred_element_type=jnp.float32).astype(jnp.bfloat16)
    weight_grad = jnp.dot(tokens.T, grad_hidden, preferred_element_type=jnp.float32).astype(jnp.bfloat16)
    return (input_grad, weight_grad)
```

```python
import functools
import math

import jax
import jax.numpy as jnp
from jax import lax
from jax.experimental import pallas as pl
from jax.experimental.pallas import tpu as pltpu
from jax.sharding import PartitionSpec as P

BF, F32 = jnp.bfloat16, jnp.float32
LIMIT = 48 * 1024 * 1024


def params(limit=LIMIT):
    return pltpu.CompilerParams(vmem_limit_bytes=limit)


def cost(flops, bytes_accessed):
    return pl.CostEstimate(flops=flops, bytes_accessed=bytes_accessed, transcendentals=0)


def place():
    row, col = lax.axis_index("row"), lax.axis_index("col")
    return row // 2, row % 2, col // 4, (col // 2) % 2, col % 2


def row_shift(value, dy, dz=0):
    pairs = [(y * 2 + z, ((y + dy) % 4) * 2 + (z + dz) % 2) for y in range(4) for z in range(2)]
    return lax.ppermute(value, "row", pairs)


def col_shift(value, dx, dh=0, dk=0):
    pairs = [
        (x * 4 + h * 2 + k, ((x + dx) % 4) * 4 + ((h + dh) % 2) * 2 + (k + dk) % 2)
        for x in range(4)
        for h in range(2)
        for k in range(2)
    ]
    return lax.ppermute(value, "col", pairs)


def slope_kernel(pre_ref, up_ref, out_ref):
    value = pre_ref[...].astype(F32)
    scale = math.sqrt(2.0 / math.pi)
    square = value * value
    tangent = jnp.tanh(scale * (value + 0.044715 * value * square))
    slope = 0.5 * (1.0 + tangent) + 0.5 * value * (1.0 - tangent * tangent) * scale * (
        1.0 + 3.0 * 0.044715 * square
    )
    out_ref[...] = (up_ref[...].astype(F32) * slope).astype(BF)


def hidden_gradient(pre_act, upstream, start, width, step=512):
    rows = pre_act.shape[0]
    spec = pl.BlockSpec((rows, step), lambda j: (0, j + start // step))
    return pl.pallas_call(
        slope_kernel,
        out_shape=jax.ShapeDtypeStruct((rows, width), BF),
        grid=(width // step,),
        in_specs=[spec, spec],
        out_specs=pl.BlockSpec((rows, step), lambda j: (0, j)),
        compiler_params=params(),
        cost_estimate=cost(30 * rows * width, 6 * rows * width),
        name="hidden_gradient",
    )(pre_act, upstream)


def transpose_kernel(*refs):
    pieces, out_ref, whole, sem = refs[:8], refs[8], refs[9], refs[10]
    _, _, x, h, core = place()
    copies = []
    for number, piece in enumerate(pieces):
        shift, other = number % 4, number // 4
        owner = (x + 4 - shift) % 4
        side = (core + other) % 2
        for dh in range(2):
            offset = (owner * 2 + (h + dh) % 2) * 128 + side * 64
            copies.append(
                pltpu.make_async_copy(
                    piece.at[dh],
                    whole.at[pl.ds(pl.multiple_of(offset, 64), 64), :],
                    sem.at[number, dh],
                )
            )
    for copy in copies:
        copy.start()
    for copy in copies:
        copy.wait()
    width = whole.shape[1]
    for start in range(0, width, 256):
        out_ref[start : start + 256, :] = whole[:, start : start + 256].T


def transposed_tokens(pieces):
    width = pieces[0].shape[2]
    rows = 1024
    return pl.pallas_call(
        transpose_kernel,
        out_shape=jax.ShapeDtypeStruct((width, rows), BF),
        in_specs=[pl.BlockSpec(memory_space=pl.ANY)] * 8,
        out_specs=pl.BlockSpec(memory_space=pltpu.VMEM),
        scratch_shapes=[pltpu.VMEM((rows, width), BF), pltpu.SemaphoreType.DMA((8, 2))],
        compiler_params=params(),
        cost_estimate=cost(0, 8 * rows * width),
        name="transposed_tokens",
    )(*pieces)


def input_kernel(blocks, *refs):
    pieces, weight_ref = refs[: 2 * blocks], refs[2 * blocks]
    own_ref, send_ref, held, sem = refs[2 * blocks + 1 :]
    core = lax.axis_index("col") % 2
    rows = 128

    @pl.when(pl.program_id(0) == 0)
    def _():
        copies = []
        for number in range(blocks):
            at = 0
            for part in range(2):
                piece = pieces[2 * number + part]
                width = piece.shape[1]
                copies.append(
                    pltpu.make_async_copy(
                        piece,
                        held.at[pl.ds(number * rows, rows), pl.ds(at, width)],
                        sem.at[number, part],
                    )
                )
                at += width
        for copy in copies:
            copy.start()
        for copy in copies:
            copy.wait()

    total = lax.dot_general(
        held[...], weight_ref[...], (((1,), (1,)), ((), ())), preferred_element_type=F32
    )
    total = total.reshape(blocks, 2, 64, total.shape[1])

    @pl.when(core == 0)
    def _():
        own_ref[...] = total[:, 0]
        send_ref[...] = total[:, 1].astype(BF)

    @pl.when(core == 1)
    def _():
        own_ref[...] = total[:, 1]
        send_ref[...] = total[:, 0].astype(BF)


def input_part(blocks, weight, step=256):
    count = len(blocks)
    features, hidden = weight.shape
    pieces = [piece for block in blocks for piece in block]
    spec = pl.BlockSpec((count, 64, step), lambda j: (0, 0, j))
    return pl.pallas_call(
        functools.partial(input_kernel, count),
        out_shape=(
            jax.ShapeDtypeStruct((count, 64, features), F32),
            jax.ShapeDtypeStruct((count, 64, features), BF),
        ),
        grid=(features // step,),
        in_specs=[pl.BlockSpec(memory_space=pl.ANY)] * (2 * count)
        + [pl.BlockSpec((step, hidden), lambda j: (j, 0))],
        out_specs=(spec, spec),
        scratch_shapes=[
            pltpu.VMEM((count * 128, hidden), BF),
            pltpu.SemaphoreType.DMA((count, 2)),
        ],
        compiler_params=params(),
        cost_estimate=cost(
            2 * count * 128 * features * hidden, 2 * features * hidden + 2 * count * 128 * hidden
        ),
        name="input_part",
    )(*pieces, weight)


def deal_kernel(groups, *refs):
    ins, outs = refs[: 2 * len(groups)], refs[2 * len(groups) : 2 * len(groups) + 4]
    both = refs[-1]
    y, _, x, _, _ = place()
    for number, group in enumerate(groups):
        own, received = ins[2 * number], ins[2 * number + 1]
        for at, dy in enumerate(group):
            both[dy] = own[at] + received[at].astype(F32)
    for dx in range(4):
        outs[dx][...] = both[(x + dx + 4 - y) % 4].astype(outs[dx].dtype)


def dealt(groups, arrays):
    rows, features = arrays[0].shape[1:]
    return pl.pallas_call(
        functools.partial(deal_kernel, groups),
        out_shape=[jax.ShapeDtypeStruct((rows, features), F32)]
        + [jax.ShapeDtypeStruct((rows, features), BF)] * 3,
        in_specs=[pl.BlockSpec(memory_space=pltpu.VMEM)] * len(arrays),
        out_specs=[pl.BlockSpec(memory_space=pltpu.VMEM)] * 4,
        scratch_shapes=[pltpu.VMEM((4, rows, features), F32)],
        compiler_params=params(),
        cost_estimate=cost(0, 40 * rows * features),
        name="dealt",
    )(*arrays)


def weight_kernel(tile, *refs):
    pieces, token_ref, out_ref, held, sem = refs[:16], refs[16], refs[17], refs[18], refs[19]
    y, z, _, _, _ = place()
    tiles = held.shape[1] // tile
    j = pl.program_id(0)

    def copies(at):
        made = []
        for number in range(8):
            dy, dz = number % 4, number // 4
            owner = ((y + dy) % 4) * 2 + (z + dz) % 2
            start = at * tile
            piece, inside = pieces[2 * number], start
            if start >= piece.shape[1]:
                piece, inside = pieces[2 * number + 1], start - piece.shape[1]
            made.append(
                pltpu.make_async_copy(
                    piece.at[:, pl.ds(inside, tile)],
                    held.at[pl.ds(pl.multiple_of(owner * 128, 128), 128), pl.ds(start, tile)],
                    sem.at[number, at],
                )
            )
        return made

    @pl.when(j == 0)
    def _():
        for at in range(tiles):
            for copy in copies(at):
                copy.start()

    for at in range(tiles):

        @pl.when(j == at)
        def _(at=at):
            for copy in copies(at):
                copy.wait()
            out_ref[...] = jnp.dot(
                token_ref[...], held[:, at * tile : (at + 1) * tile], preferred_element_type=F32
            ).astype(BF)


def weight_gradient(tokens_t, blocks, hidden, tile=512):
    features, rows = tokens_t.shape
    pieces = [piece for block in blocks for piece in block]
    return pl.pallas_call(
        functools.partial(weight_kernel, tile),
        out_shape=jax.ShapeDtypeStruct((features, hidden), BF),
        grid=(hidden // tile,),
        in_specs=[pl.BlockSpec(memory_space=pl.ANY)] * 16
        + [pl.BlockSpec((features, rows), lambda j: (0, 0))],
        out_specs=pl.BlockSpec((features, tile), lambda j: (0, j)),
        scratch_shapes=[
            pltpu.VMEM((rows, hidden), BF),
            pltpu.SemaphoreType.DMA((8, hidden // tile)),
        ],
        compiler_params=params(),
        cost_estimate=cost(2 * rows * features * hidden, 2 * features * hidden),
        name="weight_gradient",
    )(*pieces, tokens_t)


def local(tokens, weight, pre_act, upstream):
    y, z, x, h, core = place()
    hidden = pre_act.shape[1]
    first = hidden * 2 // 3
    a = hidden_gradient(pre_act, upstream, 0, first)
    b = hidden_gradient(pre_act, upstream, first, hidden - first)

    za = row_shift(a, 0, 1)
    ua, da = row_shift(a, 1), row_shift(a, -1)
    zb = row_shift(b, 0, 1)
    ub, db = row_shift(b, 1), row_shift(b, -1)
    qa, qb = row_shift(ua, 1), row_shift(db, -1)
    zua, zda = row_shift(za, 1), row_shift(za, -1)
    zub, zdb = row_shift(ub, 0, 1), row_shift(db, 0, 1)
    zqa, zqb = row_shift(zda, -1), row_shift(qb, 0, 1)

    pair = jnp.stack([tokens, col_shift(tokens, 0, 1)])
    mine = [pair] + [col_shift(pair, dx) for dx in (1, 2, 3)]
    others = [col_shift(value, 0, 0, 1) for value in mine]
    tokens_t = transposed_tokens(mine + others)

    near = [(a, b), (da, db), (qa, qb), (ua, ub)]
    far = [(za, zb), (zda, zdb), (zqa, zqb), (zua, zub)]

    own1, send1 = input_part(near, weight)
    got1 = col_shift(send1, 0, 0, 1)
    s0, s1, s2, s3 = dealt(((0, 1, 2, 3),), [own1, got1])
    r1, r2, r3 = col_shift(s1, 1), col_shift(s2, 2), col_shift(s3, 3)
    sum1 = s0 + r1.astype(F32) + r2.astype(F32) + r3.astype(F32)

    own2, send2 = input_part([far[0], far[1], far[3]], weight)
    got2 = col_shift(send2, 0, 0, 1)
    own3, send3 = input_part([far[2]], weight)
    got3 = col_shift(send3, 0, 0, 1)
    t0, t1, t2, t3 = dealt(((0, 1, 3), (2,)), [own2, got2, own3, got3])
    v1, v2, v3 = col_shift(t1, 1), col_shift(t2, 2), col_shift(t3, 3)

    weight_grad = weight_gradient(tokens_t, near + far, hidden)

    sum2 = t0 + v1.astype(F32) + v2.astype(F32) + v3.astype(F32)
    owner = h == z
    last = col_shift(jnp.where(owner, sum2, sum1).astype(BF), 0, 1)
    input_grad = (jnp.where(owner, sum1, sum2) + last.astype(F32)).astype(BF)
    return (input_grad, weight_grad)


def solution(mesh):
    in_specs = (P("col", "row"), P("row", "col"), P("row", "col"), P("row", "col"))
    out_specs = (P("col", "row"), P("row", "col"))
    return jax.shard_map(local, mesh=mesh, in_specs=in_specs, out_specs=out_specs, check_vma=False)
```

```python
import functools
import math

import jax
import jax.numpy as jnp
from jax import lax
from jax.experimental import pallas as pl
from jax.experimental.pallas import tpu as pltpu
from jax.sharding import PartitionSpec as P

BF, F32 = jnp.bfloat16, jnp.float32
LIMIT = 32 * 1024 * 1024
WHOLE = 60 * 1024 * 1024


def params(limit=LIMIT):
    return pltpu.CompilerParams(vmem_limit_bytes=limit)


def cost(flops, bytes_accessed):
    return pl.CostEstimate(
        flops=flops, bytes_accessed=bytes_accessed, transcendentals=0
    )


def place():
    row, col = lax.axis_index("row"), lax.axis_index("col")
    return row // 2, row % 2, col // 4, (col // 2) % 2, col % 2


def row_shift(value, dy, dz=0):
    pairs = [(y * 2 + z, ((y + dy) % 4) * 2 + (z + dz) % 2) for y in range(4) for z in range(2)]
    return lax.ppermute(value, "row", pairs)


def col_shift(value, dx, dh=0, dk=0):
    pairs = [
        (x * 4 + h * 2 + k, ((x + dx) % 4) * 4 + ((h + dh) % 2) * 2 + (k + dk) % 2)
        for x in range(4)
        for h in range(2)
        for k in range(2)
    ]
    return lax.ppermute(value, "col", pairs)


def after(value, *others):
    return lax.optimization_barrier((value, *others))[0]


def slope_kernel(pre_ref, up_ref, out_ref):
    value = pre_ref[...].astype(F32)
    scale = math.sqrt(2.0 / math.pi)
    square = value * value
    tangent = jnp.tanh(scale * (value + 0.044715 * value * square))
    slope = 0.5 * (1.0 + tangent) + 0.5 * value * (1.0 - tangent * tangent) * scale * (
        1.0 + 3.0 * 0.044715 * square
    )
    out_ref[...] = (up_ref[...].astype(F32) * slope).astype(BF)


def hidden_gradient(pre_act, upstream, step=1024):
    rows, width = pre_act.shape
    spec = pl.BlockSpec((rows, step), lambda j: (0, j))
    return pl.pallas_call(
        slope_kernel,
        out_shape=jax.ShapeDtypeStruct((rows, width), BF),
        grid=(width // step,),
        in_specs=[spec, spec],
        out_specs=spec,
        compiler_params=params(),
        cost_estimate=cost(30 * rows * width, 6 * rows * width),
        name="hidden_gradient",
    )(pre_act, upstream)


def transpose_kernel(*refs):
    pieces, (out_ref, whole, sem) = refs[:4], refs[4:]
    _, _, x, h, _ = place()
    copies = []
    for shift, piece in enumerate(pieces):
        owner = (x + 4 - shift) % 4
        for dh in range(2):
            offset = (owner * 2 + (h + dh) % 2) * 64
            copies.append(
                pltpu.make_async_copy(
                    piece.at[dh],
                    whole.at[pl.ds(pl.multiple_of(offset, 64), 64), :],
                    sem.at[shift, dh],
                )
            )
    for copy in copies:
        copy.start()
    for copy in copies:
        copy.wait()
    for start in range(0, whole.shape[1], 256):
        out_ref[start : start + 256, :] = whole[:, start : start + 256].T


def transposed_tokens(pieces):
    width = pieces[0].shape[2]
    rows = 8 * 64
    return pl.pallas_call(
        transpose_kernel,
        out_shape=jax.ShapeDtypeStruct((width, rows), BF),
        grid=(1,),
        in_specs=[pl.BlockSpec(memory_space=pl.ANY)] * 4,
        out_specs=pl.BlockSpec((width, rows), lambda j: (0, 0)),
        scratch_shapes=[pltpu.VMEM((rows, width), BF), pltpu.SemaphoreType.DMA((4, 2))],
        compiler_params=params(),
        cost_estimate=cost(0, 8 * rows * width),
        name="transposed_tokens",
    )(*pieces)


def hold_kernel(weight_ref, out_ref, sem):
    step = weight_ref.shape[0] // 4
    copies = [
        pltpu.make_async_copy(
            weight_ref.at[pl.ds(i * step, step), :], out_ref.at[pl.ds(i * step, step), :], sem.at[i]
        )
        for i in range(4)
    ]
    for copy in copies:
        copy.start()
    for copy in copies:
        copy.wait()


def held_weight(weight):
    return pl.pallas_call(
        hold_kernel,
        out_shape=pltpu.VMEM(weight.shape, weight.dtype),
        in_specs=[pl.BlockSpec(memory_space=pl.ANY)],
        out_specs=pl.BlockSpec(memory_space=pltpu.VMEM),
        scratch_shapes=[pltpu.SemaphoreType.DMA((4,))],
        compiler_params=params(),
        cost_estimate=cost(0, 2 * weight.size * 2),
        name="held_weight",
    )(weight)


def input_kernel(layout, *refs):
    count = len(layout)
    pieces, weight_ref, (own_ref, send_ref, held, sem) = refs[:count], refs[count], refs[count + 1 :]
    core = lax.axis_index("col") % 2

    @pl.when(pl.program_id(0) == 0)
    def _():
        copies, at = [], 0
        for number, rows in enumerate(layout):
            copies.append(
                pltpu.make_async_copy(pieces[number], held.at[pl.ds(at, rows), :], sem.at[number])
            )
            at += rows
        for copy in copies:
            copy.start()
        for copy in copies:
            copy.wait()

    step = own_ref.shape[2]
    part = weight_ref[pl.ds(pl.multiple_of(pl.program_id(0) * step, step), step), :]
    total = lax.dot_general(
        held[...], part, (((1,), (1,)), ((), ())), preferred_element_type=F32
    )
    total = total.reshape(own_ref.shape[0], 2, 64, total.shape[1])

    @pl.when(core == 0)
    def _():
        own_ref[...] = total[:, 0]
        send_ref[...] = total[:, 1].astype(BF)

    @pl.when(core == 1)
    def _():
        own_ref[...] = total[:, 1]
        send_ref[...] = total[:, 0].astype(BF)


def input_part(blocks, weight, step=768):
    count = len(blocks)
    features, hidden = weight.shape
    pieces = [piece for block in blocks for piece in block]
    layout = tuple(piece.shape[0] for piece in pieces)
    spec = pl.BlockSpec((count, 64, step), lambda j: (0, 0, j))
    return pl.pallas_call(
        functools.partial(input_kernel, layout),
        out_shape=(
            jax.ShapeDtypeStruct((count, 64, features), F32),
            jax.ShapeDtypeStruct((count, 64, features), BF),
        ),
        grid=(features // step,),
        in_specs=[pl.BlockSpec(memory_space=pl.ANY)] * len(pieces)
        + [pl.BlockSpec(memory_space=pltpu.VMEM)],
        out_specs=(spec, spec),
        scratch_shapes=[
            pltpu.VMEM((count * 128, hidden), BF),
            pltpu.SemaphoreType.DMA((len(pieces),)),
        ],
        compiler_params=params(),
        cost_estimate=cost(
            2 * count * 128 * features * hidden, 2 * features * hidden + 2 * count * 128 * hidden
        ),
        name="input_part",
    )(*pieces, weight)


def deal_kernel(places, *refs):
    count = len(places)
    ins, outs, both = refs[: 2 * count], refs[2 * count : 2 * count + 4], refs[-1]
    y, _, x, _, _ = place()
    for number, group in enumerate(places):
        own, received = ins[2 * number], ins[2 * number + 1]
        for at, dy in group:
            both[dy] = own[at] + received[at].astype(F32)
    for dx in range(4):
        outs[dx][...] = both[(x + dx + 4 - y) % 4].astype(outs[dx].dtype)


def dealt(places, arrays, limit, step=768):
    rows, features = arrays[0].shape[1:]
    spec = pl.BlockSpec((rows, step), lambda j: (0, j))
    return pl.pallas_call(
        functools.partial(deal_kernel, places),
        out_shape=[jax.ShapeDtypeStruct((rows, features), F32)]
        + [jax.ShapeDtypeStruct((rows, features), BF)] * 3,
        grid=(features // step,),
        in_specs=[
            pl.BlockSpec((array.shape[0], rows, step), lambda j: (0, 0, j)) for array in arrays
        ],
        out_specs=[spec] * 4,
        scratch_shapes=[pltpu.VMEM((4, rows, step), F32)],
        compiler_params=params(limit),
        cost_estimate=cost(0, 40 * rows * features),
        name="dealt",
    )(*arrays)


def weight_kernel(tile, first, count, halves, *refs):
    arrays = len(set(number for half in halves for number, _ in half))
    pieces, (mine_ref, other_ref) = refs[:arrays], refs[arrays : arrays + 2]
    out_ref, held, tokens, sem, token_sem = refs[-5:]
    y, z, _, _, core = place()
    j = pl.program_id(0)

    def copies(group):
        made = []
        start, width = (0, tile) if group == 0 else (tile, (count - 1) * tile)
        for block, half in enumerate(halves):
            owner = ((y + block % 4) % 4) * 2 + (z + block // 4) % 2
            for side, (number, row) in enumerate(half):
                made.append(
                    pltpu.make_async_copy(
                        pieces[number].at[pl.ds(row, 64), pl.ds(first * tile + start, width)],
                        held.at[
                            pl.ds(pl.multiple_of(side * 512 + owner * 64, 64), 64),
                            pl.ds(start, width),
                        ],
                        sem.at[block * 2 + side, group],
                    )
                )
        return made

    def token_copies():
        return [
            pltpu.make_async_copy(
                ref, tokens.at[:, pl.ds(pl.multiple_of(side * 512, 512), 512)], token_sem.at[number]
            )
            for number, (ref, side) in enumerate(((mine_ref, core), (other_ref, 1 - core)))
        ]

    @pl.when(j == 0)
    def _():
        made = token_copies() + copies(0)
        for copy in made + copies(1):
            copy.start()
        for copy in made:
            copy.wait()

    @pl.when(j == 1)
    def _():
        for copy in copies(1):
            copy.wait()

    out_ref[...] = jnp.dot(
        tokens[...],
        held[:, pl.ds(pl.multiple_of(j * tile, tile), tile)],
        preferred_element_type=F32,
    ).astype(BF)


def weight_gradient(mine, other, blocks, hidden, first, count, before=None, tile=512):
    features, rows = mine.shape[0], 2 * mine.shape[1]
    pieces = [piece for block in blocks for piece in block]
    halves, number = [], 0
    for block in blocks:
        if len(block) == 1:
            halves.append(((number, 0), (number, 64)))
        else:
            halves.append(((number, 0), (number + 1, 0)))
        number += len(block)
    operands = [*pieces, mine, other]
    aliases = {}
    if before is not None:
        aliases = {len(operands): 0}
        operands.append(before)
    return pl.pallas_call(
        functools.partial(weight_kernel, tile, first, count, tuple(halves)),
        out_shape=jax.ShapeDtypeStruct((features, hidden), BF),
        grid=(count,),
        in_specs=[pl.BlockSpec(memory_space=pl.ANY)] * len(operands),
        out_specs=pl.BlockSpec((features, tile), lambda j: (0, first + j)),
        scratch_shapes=[
            pltpu.VMEM((rows, count * tile), BF),
            pltpu.VMEM((features, rows), BF),
            pltpu.SemaphoreType.DMA((16, 2)),
            pltpu.SemaphoreType.DMA((2,)),
        ],
        input_output_aliases=aliases,
        compiler_params=params(WHOLE),
        cost_estimate=cost(3 * rows * features * count * tile, 2 * features * count * tile),
        name="weight_gradient",
    )(*operands)


def local(tokens, weight, pre_act, upstream):
    y, z, x, h, core = place()
    hidden = pre_act.shape[1]

    own = hidden_gradient(pre_act, upstream)
    up, down, across = row_shift(own, 1), row_shift(own, -1), row_shift(own, 0, 1)

    pair = jnp.stack([tokens, col_shift(tokens, 0, 1)])
    mine = [pair] + [col_shift(pair, dx) for dx in (1, 2, 3)]
    tokens_mine = transposed_tokens(mine)
    tokens_other = col_shift(tokens_mine, 0, 0, 1)

    far_y = row_shift(up, 1)
    up_z = row_shift(after(up, across), 0, 1)
    down_z = row_shift(after(across, down), -1)
    far_z = (row_shift(up_z[:64], 1), row_shift(down_z[64:], -1))

    near = [(own,), (down,), (far_y,), (up,)]
    far = [(across,), (down_z,), far_z, (up_z,)]

    weight = held_weight(weight)
    own1, send1 = input_part([near[0], near[1], near[3], far[0]], weight)
    got1 = col_shift(send1, 0, 0, 1)
    own2, send2 = input_part([near[2], far[1], far[3]], weight)
    got2 = col_shift(send2, 0, 0, 1)
    s0, s1, s2, s3 = dealt((((0, 0), (1, 1), (2, 3)), ((0, 2),)), [own1, got1, own2, got2], LIMIT)
    r1, r2, r3 = col_shift(s1, 1), col_shift(s2, 2), col_shift(s3, 3)

    own3, send3 = input_part([(after(far_z[0], s1), far_z[1])], weight)
    got3 = after(col_shift(send3, 0, 0, 1), r1, r2, r3)
    t0, t1, t2, t3 = dealt(
        (((3, 0),), ((1, 1), (2, 3)), ((0, 2),)), [own1, got1, own2, got2, own3, got3], WHOLE
    )
    v1, v2, v3 = col_shift(t1, 1), col_shift(t2, 2), col_shift(t3, 3)

    tokens_other = after(tokens_other, t1)
    weight_grad = weight_gradient(tokens_mine, tokens_other, near + far, hidden, 0, 4)
    t0, weight_grad = lax.optimization_barrier((t0, weight_grad))

    sum1 = s0 + r1.astype(F32) + r2.astype(F32) + r3.astype(F32)
    sum2 = t0 + v1.astype(F32) + v2.astype(F32) + v3.astype(F32)
    owner = h == z
    last = jnp.where(owner, sum2, sum1).astype(BF)
    last, weight_grad = lax.optimization_barrier((last, weight_grad))
    last = col_shift(last, 0, 1)
    weight_grad = weight_gradient(
        tokens_mine, tokens_other, near + far, hidden, 4, 2, weight_grad
    )
    input_grad = (jnp.where(owner, sum1, sum2) + last.astype(F32)).astype(BF)
    return (input_grad, weight_grad)


def solution(mesh):
    in_specs = (P("col", "row"), P("row", "col"), P("row", "col"), P("row", "col"))
    out_specs = (P("col", "row"), P("row", "col"))
    return jax.shard_map(local, mesh=mesh, in_specs=in_specs, out_specs=out_specs, check_vma=False)
```

```python
import functools
import math

import jax
import jax.numpy as jnp
from jax import lax
from jax.experimental import pallas as pl
from jax.experimental.pallas import tpu as pltpu
from jax.sharding import PartitionSpec as P

BF, F32 = jnp.bfloat16, jnp.float32
LIMIT = 32 * 1024 * 1024
WHOLE = 40 * 1024 * 1024


def params(limit=LIMIT):
    return pltpu.CompilerParams(vmem_limit_bytes=limit)


def cost(flops, bytes_accessed):
    return pl.CostEstimate(
        flops=flops, bytes_accessed=bytes_accessed, transcendentals=0
    )


def place():
    row, col = lax.axis_index("row"), lax.axis_index("col")
    return row // 2, row % 2, col // 4, (col // 2) % 2, col % 2


def row_shift(value, dy, dz=0):
    pairs = [(y * 2 + z, ((y + dy) % 4) * 2 + (z + dz) % 2) for y in range(4) for z in range(2)]
    return lax.ppermute(value, "row", pairs)


def col_shift(value, dx, dh=0, dk=0):
    pairs = [
        (x * 4 + h * 2 + k, ((x + dx) % 4) * 4 + ((h + dh) % 2) * 2 + (k + dk) % 2)
        for x in range(4)
        for h in range(2)
        for k in range(2)
    ]
    return lax.ppermute(value, "col", pairs)


def after(value, *others):
    return lax.optimization_barrier((value, *others))[0]


def slope_kernel(pre_ref, up_ref, out_ref):
    value = pre_ref[...].astype(F32)
    scale = math.sqrt(2.0 / math.pi)
    square = value * value
    tangent = jnp.tanh(scale * (value + 0.044715 * value * square))
    slope = 0.5 * (1.0 + tangent) + 0.5 * value * (1.0 - tangent * tangent) * scale * (
        1.0 + 3.0 * 0.044715 * square
    )
    out_ref[...] = (up_ref[...].astype(F32) * slope).astype(BF)


def hidden_gradient(pre_act, upstream, step=1024):
    rows, width = pre_act.shape
    spec = pl.BlockSpec((rows, step), lambda j: (0, j))
    return pl.pallas_call(
        slope_kernel,
        out_shape=jax.ShapeDtypeStruct((rows, width), BF),
        grid=(width // step,),
        in_specs=[spec, spec],
        out_specs=spec,
        compiler_params=params(),
        cost_estimate=cost(30 * rows * width, 6 * rows * width),
        name="hidden_gradient",
    )(pre_act, upstream)


def transpose_kernel(*refs):
    pieces, (out_ref, whole, sem) = refs[:4], refs[4:]
    _, _, x, h, _ = place()
    copies = []
    for shift, piece in enumerate(pieces):
        owner = (x + 4 - shift) % 4
        for dh in range(2):
            offset = (owner * 2 + (h + dh) % 2) * 64
            copies.append(
                pltpu.make_async_copy(
                    piece.at[dh],
                    whole.at[pl.ds(pl.multiple_of(offset, 64), 64), :],
                    sem.at[shift, dh],
                )
            )
    for copy in copies:
        copy.start()
    for copy in copies:
        copy.wait()
    for start in range(0, whole.shape[1], 256):
        out_ref[start : start + 256, :] = whole[:, start : start + 256].T


def transposed_tokens(pieces):
    width = pieces[0].shape[2]
    rows = 8 * 64
    return pl.pallas_call(
        transpose_kernel,
        out_shape=jax.ShapeDtypeStruct((width, rows), BF),
        grid=(1,),
        in_specs=[pl.BlockSpec(memory_space=pl.ANY)] * 4,
        out_specs=pl.BlockSpec((width, rows), lambda j: (0, 0)),
        scratch_shapes=[pltpu.VMEM((rows, width), BF), pltpu.SemaphoreType.DMA((4, 2))],
        compiler_params=params(),
        cost_estimate=cost(0, 8 * rows * width),
        name="transposed_tokens",
    )(*pieces)


def side_kernel(mine_ref, other_ref, out_ref, sem):
    core = lax.axis_index("col") % 2
    copies = [
        pltpu.make_async_copy(
            ref, out_ref.at[:, pl.ds(pl.multiple_of(side * 512, 512), 512)], sem.at[number]
        )
        for number, (ref, side) in enumerate(((mine_ref, core), (other_ref, 1 - core)))
    ]
    for copy in copies:
        copy.start()
    for copy in copies:
        copy.wait()


def held_tokens(mine, other):
    features, rows = mine.shape
    return pl.pallas_call(
        side_kernel,
        out_shape=pltpu.VMEM((features, 2 * rows), BF),
        in_specs=[pl.BlockSpec(memory_space=pl.ANY)] * 2,
        out_specs=pl.BlockSpec(memory_space=pltpu.VMEM),
        scratch_shapes=[pltpu.SemaphoreType.DMA((2,))],
        compiler_params=params(),
        cost_estimate=cost(0, 8 * features * rows),
        name="held_tokens",
    )(mine, other)


def hold_kernel(weight_ref, out_ref, sem):
    step = weight_ref.shape[0] // 4
    copies = [
        pltpu.make_async_copy(
            weight_ref.at[pl.ds(i * step, step), :], out_ref.at[pl.ds(i * step, step), :], sem.at[i]
        )
        for i in range(4)
    ]
    for copy in copies:
        copy.start()
    for copy in copies:
        copy.wait()


def held_weight(weight):
    return pl.pallas_call(
        hold_kernel,
        out_shape=pltpu.VMEM(weight.shape, weight.dtype),
        in_specs=[pl.BlockSpec(memory_space=pl.ANY)],
        out_specs=pl.BlockSpec(memory_space=pltpu.VMEM),
        scratch_shapes=[pltpu.SemaphoreType.DMA((4,))],
        compiler_params=params(),
        cost_estimate=cost(0, 2 * weight.size * 2),
        name="held_weight",
    )(weight)


def input_kernel(layout, *refs):
    count = len(layout)
    pieces, weight_ref, (own_ref, send_ref, held, sem) = refs[:count], refs[count], refs[count + 1 :]
    core = lax.axis_index("col") % 2

    @pl.when(pl.program_id(0) == 0)
    def _():
        copies, at = [], 0
        for number, rows in enumerate(layout):
            copies.append(
                pltpu.make_async_copy(pieces[number], held.at[pl.ds(at, rows), :], sem.at[number])
            )
            at += rows
        for copy in copies:
            copy.start()
        for copy in copies:
            copy.wait()

    step = own_ref.shape[2]
    part = weight_ref[pl.ds(pl.multiple_of(pl.program_id(0) * step, step), step), :]
    total = lax.dot_general(
        held[...], part, (((1,), (1,)), ((), ())), preferred_element_type=F32
    )
    total = total.reshape(own_ref.shape[0], 2, 64, total.shape[1])

    @pl.when(core == 0)
    def _():
        own_ref[...] = total[:, 0]
        send_ref[...] = total[:, 1].astype(BF)

    @pl.when(core == 1)
    def _():
        own_ref[...] = total[:, 1]
        send_ref[...] = total[:, 0].astype(BF)


def input_part(blocks, weight, step=768):
    count = len(blocks)
    features, hidden = weight.shape
    pieces = [piece for block in blocks for piece in block]
    layout = tuple(piece.shape[0] for piece in pieces)
    spec = pl.BlockSpec((count, 64, step), lambda j: (0, 0, j))
    return pl.pallas_call(
        functools.partial(input_kernel, layout),
        out_shape=(
            jax.ShapeDtypeStruct((count, 64, features), F32),
            jax.ShapeDtypeStruct((count, 64, features), BF),
        ),
        grid=(features // step,),
        in_specs=[pl.BlockSpec(memory_space=pl.ANY)] * len(pieces)
        + [pl.BlockSpec(memory_space=pltpu.VMEM)],
        out_specs=(spec, spec),
        scratch_shapes=[
            pltpu.VMEM((count * 128, hidden), BF),
            pltpu.SemaphoreType.DMA((len(pieces),)),
        ],
        compiler_params=params(),
        cost_estimate=cost(
            2 * count * 128 * features * hidden, 2 * features * hidden + 2 * count * 128 * hidden
        ),
        name="input_part",
    )(*pieces, weight)


def deal_kernel(order, *refs):
    count = len(order)
    ins, outs, both = refs[: 2 * count], refs[2 * count : 2 * count + 4], refs[-1]
    y, _, x, _, _ = place()
    for number, dy in enumerate(order):
        both[dy] = ins[2 * number][0] + ins[2 * number + 1][0].astype(F32)
    for dx in range(4):
        outs[dx][...] = both[(x + dx + 4 - y) % 4].astype(outs[dx].dtype)


def dealt(blocks, limit, step=768):
    rows, features = blocks[0][0].shape[1:]
    spec = pl.BlockSpec((rows, step), lambda j: (0, j))
    arrays, specs = [], []
    for own, received, at in blocks:
        arrays += [own, received]
        specs += [pl.BlockSpec((1, rows, step), lambda j, at=at: (at, 0, j))] * 2
    return pl.pallas_call(
        functools.partial(deal_kernel, range(len(blocks))),
        out_shape=[jax.ShapeDtypeStruct((rows, features), F32)]
        + [jax.ShapeDtypeStruct((rows, features), BF)] * 3,
        grid=(features // step,),
        in_specs=specs,
        out_specs=[spec] * 4,
        scratch_shapes=[pltpu.VMEM((4, rows, step), F32)],
        compiler_params=params(limit),
        cost_estimate=cost(0, 40 * rows * features),
        name="dealt",
    )(*arrays)


def rows_kernel(halves, *refs):
    pieces, (out_ref, sem) = refs[:-2], refs[-2:]
    y, z, _, _, _ = place()
    copies = []
    for block, half in enumerate(halves):
        owner = ((y + block % 4) % 4) * 2 + (z + block // 4) % 2
        for side, (number, row) in enumerate(half):
            copies.append(
                pltpu.make_async_copy(
                    pieces[number].at[pl.ds(row, 64), :],
                    out_ref.at[pl.ds(pl.multiple_of(side * 512 + owner * 64, 64), 64), :],
                    sem.at[block * 2 + side],
                )
            )
    for copy in copies:
        copy.start()
    for copy in copies:
        copy.wait()


def held_rows(blocks):
    pieces = [piece for block in blocks for piece in block]
    halves, number = [], 0
    for block in blocks:
        if len(block) == 1:
            halves.append(((number, 0), (number, 64)))
        else:
            halves.append(((number, 0), (number + 1, 0)))
        number += len(block)
    rows, hidden = len(blocks) * 128, pieces[0].shape[1]
    return pl.pallas_call(
        functools.partial(rows_kernel, tuple(halves)),
        out_shape=pltpu.VMEM((rows, hidden), BF),
        in_specs=[pl.BlockSpec(memory_space=pl.ANY)] * len(pieces),
        out_specs=pl.BlockSpec(memory_space=pltpu.VMEM),
        scratch_shapes=[pltpu.SemaphoreType.DMA((16,))],
        compiler_params=params(52 * 1024 * 1024),
        cost_estimate=cost(0, 4 * rows * hidden),
        name="held_rows",
    )(*pieces)


def weight_kernel(tile, first, tokens, held, *refs):
    columns = pl.ds(pl.multiple_of((first + pl.program_id(0)) * tile, tile), tile)
    refs[-1][...] = jnp.dot(
        tokens[...], held[:, columns], preferred_element_type=F32
    ).astype(BF)


def weight_gradient(tokens, held, first, count, before=None, tile=512):
    features, rows = tokens.shape
    hidden = held.shape[1]
    operands, aliases = [tokens, held], {}
    specs = [pl.BlockSpec(memory_space=pltpu.VMEM)] * 2
    if before is not None:
        aliases = {len(operands): 0}
        operands.append(before)
        specs.append(pl.BlockSpec(memory_space=pl.ANY))
    return pl.pallas_call(
        functools.partial(weight_kernel, tile, first),
        out_shape=jax.ShapeDtypeStruct((features, hidden), BF),
        grid=(count,),
        in_specs=specs,
        out_specs=pl.BlockSpec((features, tile), lambda j: (0, first + j)),
        input_output_aliases=aliases,
        compiler_params=params(LIMIT),
        cost_estimate=cost(3 * rows * features * count * tile, 2 * features * count * tile),
        name="weight_gradient",
    )(*operands)


def local(tokens, weight, pre_act, upstream):
    y, z, x, h, core = place()

    own = hidden_gradient(pre_act, upstream)
    up, down, across = row_shift(own, 1), row_shift(own, -1), row_shift(own, 0, 1)

    pair = jnp.stack([tokens, col_shift(tokens, 0, 1)])
    mine = [pair] + [col_shift(pair, dx) for dx in (1, 2, 3)]
    tokens_mine = transposed_tokens(mine)
    tokens_other = col_shift(tokens_mine, 0, 0, 1)

    far_y = row_shift(up, 1)
    up_z = row_shift(after(up, across), 0, 1)
    down_z = row_shift(after(across, down), -1)
    far_z = (row_shift(up_z[:64], 1), row_shift(down_z[64:], -1))

    near = [(own,), (down,), (far_y,), (up,)]
    far = [(across,), (down_z,), far_z, (up_z,)]

    weight = held_weight(weight)
    own1, send1 = input_part([near[0], near[1], near[3], far[0]], weight)
    got1 = col_shift(send1, 0, 0, 1)
    own2, send2 = input_part([near[2], far[1], far[3]], weight)
    got2 = col_shift(send2, 0, 0, 1)
    s0, s1, s2, s3 = dealt(
        ((own1, got1, 0), (own1, got1, 1), (own2, got2, 0), (own1, got1, 2)), LIMIT
    )
    r1, r2, r3 = col_shift(s1, 1), col_shift(s2, 2), col_shift(s3, 3)

    tokens_all = held_tokens(tokens_mine, tokens_other)
    own3, send3 = input_part([(after(far_z[0], s1, tokens_all), far_z[1])], weight)
    held = held_rows([(after(own, own3),), *near[1:], *far])
    got3 = after(col_shift(send3, 0, 0, 1), r1, r2, r3)
    t0, t1, t2, t3 = dealt(
        ((own1, got1, 3), (own2, got2, 1), (own3, got3, 0), (own2, got2, 2)), WHOLE
    )
    v1, v2, v3 = col_shift(t1, 1), col_shift(t2, 2), col_shift(t3, 3)

    tokens_all = after(tokens_all, t1)
    weight_grad = weight_gradient(tokens_all, held, 0, 4)
    t0, weight_grad = lax.optimization_barrier((t0, weight_grad))

    sum1 = s0 + r1.astype(F32) + r2.astype(F32) + r3.astype(F32)
    sum2 = t0 + v1.astype(F32) + v2.astype(F32) + v3.astype(F32)
    owner = h == z
    last = jnp.where(owner, sum2, sum1).astype(BF)
    last, weight_grad = lax.optimization_barrier((last, weight_grad))
    last = col_shift(last, 0, 1)
    weight_grad = weight_gradient(tokens_all, held, 4, 2, weight_grad)
    input_grad = (jnp.where(owner, sum1, sum2) + last.astype(F32)).astype(BF)
    return (input_grad, weight_grad)


def solution(mesh):
    in_specs = (P("col", "row"), P("row", "col"), P("row", "col"), P("row", "col"))
    out_specs = (P("col", "row"), P("row", "col"))
    return jax.shard_map(local, mesh=mesh, in_specs=in_specs, out_specs=out_specs, check_vma=False)
```

```python
import functools
import math

import jax
import jax.numpy as jnp
from jax import lax
from jax.experimental import pallas as pl
from jax.experimental.pallas import tpu as pltpu
from jax.sharding import PartitionSpec as P

BF, F32 = jnp.bfloat16, jnp.float32
LIMIT = 32 * 1024 * 1024
WHOLE = 40 * 1024 * 1024


def params(limit=LIMIT):
    return pltpu.CompilerParams(vmem_limit_bytes=limit)


def cost(flops, bytes_accessed):
    return pl.CostEstimate(
        flops=flops, bytes_accessed=bytes_accessed, transcendentals=0
    )


def place():
    row, col = lax.axis_index("row"), lax.axis_index("col")
    return row // 2, row % 2, col // 4, (col // 2) % 2, col % 2


def row_shift(value, dy, dz=0):
    pairs = [(y * 2 + z, ((y + dy) % 4) * 2 + (z + dz) % 2) for y in range(4) for z in range(2)]
    return lax.ppermute(value, "row", pairs)


def col_shift(value, dx, dh=0, dk=0):
    pairs = [
        (x * 4 + h * 2 + k, ((x + dx) % 4) * 4 + ((h + dh) % 2) * 2 + (k + dk) % 2)
        for x in range(4)
        for h in range(2)
        for k in range(2)
    ]
    return lax.ppermute(value, "col", pairs)


def after(value, *others):
    return lax.optimization_barrier((value, *others))[0]


def slope_kernel(pre_ref, up_ref, out_ref):
    value = pre_ref[...].astype(F32)
    scale = math.sqrt(2.0 / math.pi)
    square = value * value
    tangent = jnp.tanh(scale * (value + 0.044715 * value * square))
    slope = 0.5 * (1.0 + tangent) + 0.5 * value * (1.0 - tangent * tangent) * scale * (
        1.0 + 3.0 * 0.044715 * square
    )
    out_ref[...] = (up_ref[...].astype(F32) * slope).astype(BF)


def hidden_gradient(pre_act, upstream, step=1024):
    rows, width = pre_act.shape
    spec = pl.BlockSpec((rows, step), lambda j: (0, j))
    return pl.pallas_call(
        slope_kernel,
        out_shape=jax.ShapeDtypeStruct((rows, width), BF),
        grid=(width // step,),
        in_specs=[spec, spec],
        out_specs=spec,
        compiler_params=params(),
        cost_estimate=cost(30 * rows * width, 6 * rows * width),
        name="hidden_gradient",
    )(pre_act, upstream)


def transpose_kernel(*refs):
    pieces, (out_ref, whole, sem) = refs[:4], refs[4:]
    _, _, x, h, _ = place()
    copies = []
    for shift, piece in enumerate(pieces):
        owner = (x + 4 - shift) % 4
        for dh in range(2):
            offset = (owner * 2 + (h + dh) % 2) * 64
            copies.append(
                pltpu.make_async_copy(
                    piece.at[dh],
                    whole.at[pl.ds(pl.multiple_of(offset, 64), 64), :],
                    sem.at[shift, dh],
                )
            )
    for copy in copies:
        copy.start()
    for copy in copies:
        copy.wait()
    for start in range(0, whole.shape[1], 256):
        out_ref[start : start + 256, :] = whole[:, start : start + 256].T


def transposed_tokens(pieces):
    width = pieces[0].shape[2]
    rows = 8 * 64
    return pl.pallas_call(
        transpose_kernel,
        out_shape=jax.ShapeDtypeStruct((width, rows), BF),
        grid=(1,),
        in_specs=[pl.BlockSpec(memory_space=pl.ANY)] * 4,
        out_specs=pl.BlockSpec((width, rows), lambda j: (0, 0)),
        scratch_shapes=[pltpu.VMEM((rows, width), BF), pltpu.SemaphoreType.DMA((4, 2))],
        compiler_params=params(),
        cost_estimate=cost(0, 8 * rows * width),
        name="transposed_tokens",
    )(*pieces)


def side_kernel(mine_ref, other_ref, out_ref, sem):
    core = lax.axis_index("col") % 2
    copies = [
        pltpu.make_async_copy(
            ref, out_ref.at[:, pl.ds(pl.multiple_of(side * 512, 512), 512)], sem.at[number]
        )
        for number, (ref, side) in enumerate(((mine_ref, core), (other_ref, 1 - core)))
    ]
    for copy in copies:
        copy.start()
    for copy in copies:
        copy.wait()


def held_tokens(mine, other):
    features, rows = mine.shape
    return pl.pallas_call(
        side_kernel,
        out_shape=pltpu.VMEM((features, 2 * rows), BF),
        in_specs=[pl.BlockSpec(memory_space=pl.ANY)] * 2,
        out_specs=pl.BlockSpec(memory_space=pltpu.VMEM),
        scratch_shapes=[pltpu.SemaphoreType.DMA((2,))],
        compiler_params=params(),
        cost_estimate=cost(0, 8 * features * rows),
        name="held_tokens",
    )(mine, other)


def hold_kernel(weight_ref, out_ref, sem):
    step = weight_ref.shape[0] // 4
    copies = [
        pltpu.make_async_copy(
            weight_ref.at[pl.ds(i * step, step), :], out_ref.at[pl.ds(i * step, step), :], sem.at[i]
        )
        for i in range(4)
    ]
    for copy in copies:
        copy.start()
    for copy in copies:
        copy.wait()


def held_weight(weight):
    return pl.pallas_call(
        hold_kernel,
        out_shape=pltpu.VMEM(weight.shape, weight.dtype),
        in_specs=[pl.BlockSpec(memory_space=pl.ANY)],
        out_specs=pl.BlockSpec(memory_space=pltpu.VMEM),
        scratch_shapes=[pltpu.SemaphoreType.DMA((4,))],
        compiler_params=params(),
        cost_estimate=cost(0, 2 * weight.size * 2),
        name="held_weight",
    )(weight)


def input_kernel(layout, *refs):
    count = len(layout)
    pieces, weight_ref, (own_ref, send_ref, held, sem) = refs[:count], refs[count], refs[count + 1 :]
    core = lax.axis_index("col") % 2

    @pl.when(pl.program_id(0) == 0)
    def _():
        copies, at = [], 0
        for number, rows in enumerate(layout):
            copies.append(
                pltpu.make_async_copy(pieces[number], held.at[pl.ds(at, rows), :], sem.at[number])
            )
            at += rows
        for copy in copies:
            copy.start()
        for copy in copies:
            copy.wait()

    step = own_ref.shape[2]
    part = weight_ref[pl.ds(pl.multiple_of(pl.program_id(0) * step, step), step), :]
    total = lax.dot_general(
        held[...], part, (((1,), (1,)), ((), ())), preferred_element_type=F32
    )
    total = total.reshape(own_ref.shape[0], 2, 64, total.shape[1])

    @pl.when(core == 0)
    def _():
        own_ref[...] = total[:, 0]
        send_ref[...] = total[:, 1].astype(BF)

    @pl.when(core == 1)
    def _():
        own_ref[...] = total[:, 1]
        send_ref[...] = total[:, 0].astype(BF)


def input_part(blocks, weight, step=768):
    count = len(blocks)
    features, hidden = weight.shape
    pieces = [piece for block in blocks for piece in block]
    layout = tuple(piece.shape[0] for piece in pieces)
    spec = pl.BlockSpec((count, 64, step), lambda j: (0, 0, j))
    return pl.pallas_call(
        functools.partial(input_kernel, layout),
        out_shape=(
            jax.ShapeDtypeStruct((count, 64, features), F32),
            jax.ShapeDtypeStruct((count, 64, features), BF),
        ),
        grid=(features // step,),
        in_specs=[pl.BlockSpec(memory_space=pl.ANY)] * len(pieces)
        + [pl.BlockSpec(memory_space=pltpu.VMEM)],
        out_specs=(spec, spec),
        scratch_shapes=[
            pltpu.VMEM((count * 128, hidden), BF),
            pltpu.SemaphoreType.DMA((len(pieces),)),
        ],
        compiler_params=params(),
        cost_estimate=cost(
            2 * count * 128 * features * hidden, 2 * features * hidden + 2 * count * 128 * hidden
        ),
        name="input_part",
    )(*pieces, weight)


def deal_kernel(order, *refs):
    count = len(order)
    ins, outs, both = refs[: 2 * count], refs[2 * count : 2 * count + 4], refs[-1]
    y, _, x, _, _ = place()
    for number, dy in enumerate(order):
        both[dy] = ins[2 * number][0] + ins[2 * number + 1][0].astype(F32)
    for dx in range(4):
        outs[dx][...] = both[(x + dx + 4 - y) % 4].astype(outs[dx].dtype)


def dealt(blocks, limit, step=768):
    rows, features = blocks[0][0].shape[1:]
    spec = pl.BlockSpec((rows, step), lambda j: (0, j))
    arrays, specs = [], []
    for own, received, at in blocks:
        arrays += [own, received]
        specs += [pl.BlockSpec((1, rows, step), lambda j, at=at: (at, 0, j))] * 2
    return pl.pallas_call(
        functools.partial(deal_kernel, range(len(blocks))),
        out_shape=[jax.ShapeDtypeStruct((rows, features), F32)]
        + [jax.ShapeDtypeStruct((rows, features), BF)] * 3,
        grid=(features // step,),
        in_specs=specs,
        out_specs=[spec] * 4,
        scratch_shapes=[pltpu.VMEM((4, rows, step), F32)],
        compiler_params=params(limit),
        cost_estimate=cost(0, 40 * rows * features),
        name="dealt",
    )(*arrays)


def rows_kernel(halves, *refs):
    pieces, (out_ref, sem) = refs[:-2], refs[-2:]
    y, z, _, _, _ = place()
    copies = []
    for block, half in enumerate(halves):
        owner = ((y + block % 4) % 4) * 2 + (z + block // 4) % 2
        for side, (number, row) in enumerate(half):
            copies.append(
                pltpu.make_async_copy(
                    pieces[number].at[pl.ds(row, 64), :],
                    out_ref.at[pl.ds(pl.multiple_of(side * 512 + owner * 64, 64), 64), :],
                    sem.at[block * 2 + side],
                )
            )
    for copy in copies:
        copy.start()
    for copy in copies:
        copy.wait()


def held_rows(blocks):
    pieces = [piece for block in blocks for piece in block]
    halves, number = [], 0
    for block in blocks:
        if len(block) == 1:
            halves.append(((number, 0), (number, 64)))
        else:
            halves.append(((number, 0), (number + 1, 0)))
        number += len(block)
    rows, hidden = len(blocks) * 128, pieces[0].shape[1]
    return pl.pallas_call(
        functools.partial(rows_kernel, tuple(halves)),
        out_shape=pltpu.VMEM((rows, hidden), BF),
        in_specs=[pl.BlockSpec(memory_space=pl.ANY)] * len(pieces),
        out_specs=pl.BlockSpec(memory_space=pltpu.VMEM),
        scratch_shapes=[pltpu.SemaphoreType.DMA((16,))],
        compiler_params=params(52 * 1024 * 1024),
        cost_estimate=cost(0, 4 * rows * hidden),
        name="held_rows",
    )(*pieces)


def weight_kernel(tile, first, tokens, held, *refs):
    columns = pl.ds(pl.multiple_of((first + pl.program_id(0)) * tile, tile), tile)
    refs[-1][...] = jnp.dot(
        tokens[...], held[:, columns], preferred_element_type=F32
    ).astype(BF)


def weight_gradient(tokens, held, first, count, before=None, tile=512):
    features, rows = tokens.shape
    hidden = held.shape[1]
    operands, aliases = [tokens, held], {}
    specs = [pl.BlockSpec(memory_space=pltpu.VMEM)] * 2
    if before is not None:
        aliases = {len(operands): 0}
        operands.append(before)
        specs.append(pl.BlockSpec(memory_space=pl.ANY))
    return pl.pallas_call(
        functools.partial(weight_kernel, tile, first),
        out_shape=jax.ShapeDtypeStruct((features, hidden), BF),
        grid=(count,),
        in_specs=specs,
        out_specs=pl.BlockSpec((features, tile), lambda j: (0, first + j)),
        input_output_aliases=aliases,
        compiler_params=params(LIMIT),
        cost_estimate=cost(3 * rows * features * count * tile, 2 * features * count * tile),
        name="weight_gradient",
    )(*operands)


def local(tokens, weight, pre_act, upstream):
    y, z, x, h, core = place()

    own = hidden_gradient(pre_act, upstream)
    up, down, across = row_shift(own, 1), row_shift(own, -1), row_shift(own, 0, 1)

    pair = jnp.stack([tokens, col_shift(tokens, 0, 1)])
    mine = [pair] + [col_shift(pair, dx) for dx in (1, 2, 3)]
    tokens_mine = transposed_tokens(mine)
    tokens_other = col_shift(tokens_mine, 0, 0, 1)

    far_y = row_shift(up, 1)
    up_z = row_shift(after(up, across), 0, 1)
    down_z = row_shift(after(across, down), -1)
    far_z = (row_shift(up_z[:64], 1), row_shift(down_z[64:], -1))

    near = [(own,), (down,), (far_y,), (up,)]
    far = [(across,), (down_z,), far_z, (up_z,)]

    weight = held_weight(weight)
    own1, send1 = input_part([near[0], near[1], near[3], far[0]], weight)
    got1 = col_shift(send1, 0, 0, 1)
    own2, send2 = input_part([near[2], far[1], far[3]], weight)
    got2 = col_shift(send2, 0, 0, 1)
    s0, s1, s2, s3 = dealt(
        ((own1, got1, 0), (own1, got1, 1), (own2, got2, 0), (own1, got1, 2)), LIMIT
    )
    r1, r2, r3 = col_shift(s1, 1), col_shift(s2, 2), col_shift(s3, 3)

    tokens_all = held_tokens(tokens_mine, tokens_other)
    own3, send3 = input_part([(after(far_z[0], s1, tokens_all), far_z[1])], weight)
    held = held_rows([(after(own, own3),), *near[1:], *far])
    got3 = after(col_shift(send3, 0, 0, 1), r1, r2, r3)
    t0, t1, t2, t3 = dealt(
        ((own1, got1, 3), (own2, got2, 1), (own3, got3, 0), (own2, got2, 2)), WHOLE
    )
    v1, v2, v3 = col_shift(t1, 1), col_shift(t2, 2), col_shift(t3, 3)

    tokens_all = after(tokens_all, t1)
    weight_grad = weight_gradient(tokens_all, held, 0, 4)
    t0, weight_grad = lax.optimization_barrier((t0, weight_grad))

    sum1 = s0 + r1.astype(F32) + r2.astype(F32) + r3.astype(F32)
    sum2 = t0 + v1.astype(F32) + v2.astype(F32) + v3.astype(F32)
    owner = h == z
    last = jnp.where(owner, sum2, sum1).astype(BF)
    last, weight_grad = lax.optimization_barrier((last, weight_grad))
    last = col_shift(last, 0, 1)
    weight_grad = weight_gradient(tokens_all, held, 4, 2, weight_grad)
    kept = lax.optimization_barrier(jnp.where(owner, sum1, sum2))
    input_grad = (kept + last.astype(F32)).astype(BF)
    return (input_grad, weight_grad)


def solution(mesh):
    in_specs = (P("col", "row"), P("row", "col"), P("row", "col"), P("row", "col"))
    out_specs = (P("col", "row"), P("row", "col"))
    return jax.shard_map(local, mesh=mesh, in_specs=in_specs, out_specs=out_specs, check_vma=False)
```
